256 devices in a mesh: row: 16 (over y_hi, x, core), col: 16 (over y_lo, z).
Axes of the slice: x: 4, y: 4 (y_hi: 2, y_lo: 2; y = y_hi * 2 + y_lo), z: 8, core: 2. Of those that a mesh axis runs over, the one named last changes fastest.
Arguments:
- a_stored: float32 [4096, 65536], P('row', 'col'), may hold values from -6 to 6
- b_stored: float32 [65536, 4096], P('row', 'col'), may hold values from -0.0546875 to 0.0546875
Outputs:
- product: float32 [4096, 4096], P('row', 'col')
The draws below stay inside these ranges and needn't reach their ends.
All inputs are finite; a program needn't handle non-finite values.
Results may differ from the reference program's by a relative error of at most 0.0003.
Values sent between devices are 32-bit elements; how exact they have to be, the bound alone decides.
No kernel may reach another device: no remote copies, remote signals or barrier semaphores. Data moves between devices by JAX's collectives and lax.ppermute only.
A program may use at most 128 MiB of HBM per device.

```python
import jax
import jax.numpy as jnp
from jax import lax

ORDER = 65536
PANEL = 4096
CBLK = 128
RDEV = 256
STEPS = 2
KBLK = 16
ROWS = 4096
N_ROW = 16
N_COL = 16


def levels(rng, shape, split, low, top_value):
    def one(axis_at, parts):
        steps = jax.random.uniform(jax.random.fold_in(jax.random.fold_in(rng, 6), axis_at), (parts,), jnp.float32, low / len(split), top_value / len(split))
        return jnp.repeat(jnp.exp(steps), shape[axis_at] // parts).reshape((-1,) + (1,) * (len(shape) - axis_at - 1))

    factor_of = one(*split[0])
    for cut in split[1:]:
        factor_of = factor_of * one(*cut)
    return factor_of


def scatter_about(key, dims, spread, most, shards=(), kind=jnp.bfloat16):
    drawn = jax.random.normal(key, dims, jnp.float32) * spread
    if len(shards) > 0:
        drawn = levels(key, dims, shards, -0.22, 0.18) * drawn
    return jnp.clip(drawn, min=-most, max=most).astype(kind)


def setup_inputs(seed: int = 0) -> dict:
    key_of = jax.random.split(jax.random.key(seed), 3)
    a_stored = scatter_about(key_of[0], (ROWS, ORDER), 1.0, 6.0, ((0, 16), (1, 16)), jnp.float32)
    b_stored = scatter_about(key_of[1], (ORDER, PANEL), ((STEPS + 1) * ORDER // KBLK) ** -0.5, 0.0546875, ((0, 16), (1, 16)), jnp.float32)
    return {"a_stored": a_stored, "b_stored": b_stored}


def reference(a_stored, b_stored):
    rows = RDEV * N_ROW
    a_full = a_stored.reshape(rows, N_COL, ORDER // (N_COL * CBLK), CBLK).transpose(0, 2, 1, 3).reshape(rows, ORDER)
    b_full = b_stored.reshape(N_ROW, ORDER // (N_ROW * CBLK), CBLK, PANEL).transpose(1, 0, 2, 3).reshape(ORDER, PANEL)
    width = ORDER // KBLK
    columns = PANEL // N_COL

    def block_product(flat):
        row_block = flat // N_COL
        col_block = flat % N_COL
        a_rows = lax.dynamic_slice_in_dim(a_full, (row_block * RDEV).astype(jnp.int32), RDEV, 0)
        b_cols = lax.dynamic_slice_in_dim(b_full, (col_block * columns).astype(jnp.int32), columns, 1)
        total = jnp.zeros((RDEV, columns), jnp.float32)
        for offset in range(STEPS + 1):
            kblock = ((row_block + col_block + offset) % KBLK).astype(jnp.int32)
            a_part = lax.dynamic_slice_in_dim(a_rows, (kblock * width).astype(jnp.int32), width, 1)
            b_part = lax.dynamic_slice_in_dim(b_cols, (kblock * width).astype(jnp.int32), width, 0)
            total = total + jnp.dot(a_part, b_part, precision=lax.Precision.HIGHEST, preferred_element_type=jnp.float32)
        return total

    blocks = lax.map(block_product, jnp.arange(N_ROW * N_COL, dtype=jnp.int32))
    return blocks.reshape(N_ROW, N_COL, RDEV, columns).transpose(0, 2, 1, 3).reshape(rows, PANEL)
```

```python
import functools

import jax
import jax.numpy as jnp
from jax import lax
from jax.experimental import pallas as pl
from jax.experimental.pallas import tpu as pltpu
from jax.sharding import PartitionSpec as P

CBLK = 128
PIECES = 1


def order_body(shift_ref, in_ref, *out_refs):
    del shift_ref
    height = in_ref.shape[0] // len(out_refs)
    for q, out_ref in enumerate(out_refs):
        out_ref[0] = in_ref[q * height : (q + 1) * height, :]


def order_for_rows(b_stored, shift, blocks, pieces):
    height, cols = b_stored.shape
    deep = height // blocks
    part = deep // pieces
    return pl.pallas_call(
        order_body,
        grid_spec=pltpu.PrefetchScalarGridSpec(
            num_scalar_prefetch=1,
            grid=(blocks,),
            in_specs=[pl.BlockSpec((deep, cols), lambda d, shift: ((d + shift[0]) % blocks, 0))],
            out_specs=[pl.BlockSpec((1, part, cols), lambda d, shift: (d, 0, 0))] * pieces,
        ),
        out_shape=[jax.ShapeDtypeStruct((blocks, part, cols), jnp.float32)] * pieces,
        name="order_panel",
    )(shift, b_stored)


def split(value):
    high = value.astype(jnp.bfloat16)
    low = (value - high.astype(jnp.float32)).astype(jnp.bfloat16)
    return high, low


def product_body(blocks, pieces, row_ref, a_ref, *refs):
    panels, out_ref, a_high, a_low = refs[: 3 * pieces], refs[-3], refs[-2], refs[-1]
    j = pl.program_id(0)
    deep = a_ref.shape[1] // blocks

    @pl.when(j == 0)
    def _():
        for k in range(blocks):
            high, low = split(a_ref[:, k * deep : (k + 1) * deep])
            a_high[k] = high
            a_low[k] = low

    total = jnp.zeros(out_ref.shape[1:], jnp.float32)
    dot = functools.partial(jnp.dot, preferred_element_type=jnp.float32)
    for s in range(3):
        k = (row_ref[0] + j + s) % blocks
        panel = jnp.concatenate([ref[0] for ref in panels[s * pieces : (s + 1) * pieces]], axis=0)
        high, low = split(panel)
        total += dot(a_high[k], high) + (dot(a_high[k], low) + dot(a_low[k], high))
    out_ref[0] = total


def partial_products(row_index, a_stored, panels, pieces):
    blocks, part, cols = panels[0].shape
    rows, width = a_stored.shape
    deep = width // blocks
    return pl.pallas_call(
        functools.partial(product_body, blocks, pieces),
        grid_spec=pltpu.PrefetchScalarGridSpec(
            num_scalar_prefetch=1,
            grid=(blocks,),
            in_specs=[pl.BlockSpec((rows, width), lambda j, row: (0, 0))]
            + [pl.BlockSpec((1, part, cols), lambda j, row: (j, 0, 0))] * len(panels),
            out_specs=pl.BlockSpec((1, rows, cols), lambda j, row: (j, 0, 0)),
            scratch_shapes=[pltpu.VMEM((blocks, rows, deep), jnp.bfloat16)] * 2,
        ),
        out_shape=jax.ShapeDtypeStruct((blocks, rows, cols), jnp.float32),
        compiler_params=pltpu.CompilerParams(vmem_limit_bytes=40 * 2**20),
        name="partial_products",
    )(row_index, a_stored, *panels)


def shift_rows(block, distance):
    n = lax.axis_size("row")
    return lax.ppermute(block, "row", [((i - distance) % n, i) for i in range(n)])


def on_device(a_stored, b_stored):
    blocks = lax.axis_size("row")
    row_index = lax.axis_index("row").astype(jnp.int32)
    col_index = lax.axis_index("col").astype(jnp.int32)
    outgoing = order_for_rows(b_stored, (col_index + 1).reshape(1), blocks, PIECES)
    behind, own, ahead = [], [], []
    for piece in outgoing:
        piece = lax.all_to_all(piece, "row", split_axis=0, concat_axis=0, tiled=True)
        piece = lax.all_to_all(piece, "col", split_axis=0, concat_axis=0, tiled=True)
        own.append(piece)
        behind.append(shift_rows(piece, 1))
        ahead.append(shift_rows(piece, -1))
    partial = partial_products(row_index.reshape(1), a_stored, behind + own + ahead, PIECES)
    return lax.psum_scatter(partial, "col", scatter_dimension=0, tiled=True).reshape(partial.shape[1:])


def solution(mesh):
    return jax.shard_map(
        on_device,
        mesh=mesh,
        in_specs=(P("row", "col"), P("row", "col")),
        out_specs=P("row", "col"),
        check_vma=False,
    )
```

```python
import functools

import jax
import jax.numpy as jnp
import numpy as np
from jax import lax
from jax.experimental import pallas as pl
from jax.experimental.pallas import tpu as pltpu
from jax.sharding import Mesh
from jax.sharding import PartitionSpec as P

AXES = ("y_hi", "x", "core", "y_lo", "z")
ROW, COL = AXES[:3], AXES[3:]
WINDOW = 3
OFFSETS = (4, -3, 3, -2, 2, -1, 1, 0)
GROUPS = (2, 2, 4)
EARLY = 7
LARGE = 60 * 2**20
SMALL = 16 * 2**20


def order_body(along, index_ref, in_ref, *refs):
    out_refs, (held, in_sems, out_sems) = refs[:-3], refs[-3:]
    count, deep = held.shape[0], held.shape[1 + along]

    def bring(d):
        span = pl.ds(pl.multiple_of(index_ref[d] * deep, deep), deep)
        part = in_ref.at[span, :] if along == 0 else in_ref.at[:, span]
        return pltpu.make_async_copy(part, held.at[d], in_sems.at[d])

    places = [(out_ref, d) for out_ref in out_refs for d in range(out_ref.shape[0])]
    puts = [pltpu.make_async_copy(held.at[d], out.at[e], out_sems.at[d]) for d, (out, e) in enumerate(places)]
    for d in range(count):
        bring(d).start()
    for d in range(count):
        bring(d).wait()
        puts[d].start()
    for put in puts:
        put.wait()


def order_blocks(stored, index, deep, along, parts, name, room=LARGE):
    count = index.shape[0]
    shape = (deep, stored.shape[1]) if along == 0 else (stored.shape[0], deep)
    return pl.pallas_call(
        functools.partial(order_body, along),
        in_specs=[pl.BlockSpec(memory_space=pltpu.SMEM), pl.BlockSpec(memory_space=pl.ANY)],
        out_specs=[pl.BlockSpec(memory_space=pl.ANY)] * len(parts),
        out_shape=[jax.ShapeDtypeStruct((part, *shape), jnp.float32) for part in parts],
        scratch_shapes=[
            pltpu.VMEM((count, *shape), jnp.float32),
            pltpu.SemaphoreType.DMA((count,)),
            pltpu.SemaphoreType.DMA((count,)),
        ],
        name=name,
        compiler_params=pltpu.CompilerParams(vmem_limit_bytes=room),
        cost_estimate=pl.CostEstimate(flops=0, bytes_accessed=8 * count * shape[0] * shape[1], transcendentals=0),
    )(index, stored)


def split(value):
    high = value.astype(jnp.bfloat16)
    low = (value - high.astype(jnp.float32)).astype(jnp.bfloat16)
    return high, low


def split_stored_body(index_ref, in_ref, high_ref, low_ref):
    del index_ref
    high_ref[0], low_ref[0] = split(in_ref[...])


def split_stored(a_stored, index, deep):
    count, rows = index.shape[0], a_stored.shape[0]
    out = jax.ShapeDtypeStruct((count, rows, deep), jnp.bfloat16)
    out_spec = pl.BlockSpec((1, rows, deep), lambda g, index: (g, 0, 0))
    return pl.pallas_call(
        split_stored_body,
        grid_spec=pltpu.PrefetchScalarGridSpec(
            num_scalar_prefetch=1,
            grid=(count,),
            in_specs=[pl.BlockSpec((rows, deep), lambda g, index: (0, index[g]))],
            out_specs=[out_spec, out_spec],
        ),
        out_shape=[out, out],
        name="split_stored",
        compiler_params=pltpu.CompilerParams(vmem_limit_bytes=LARGE),
        cost_estimate=pl.CostEstimate(flops=0, bytes_accessed=8 * count * rows * deep, transcendentals=0),
    )(index, a_stored)


def split_blocks_body(cut, one_ref, two_ref, high_ref, low_ref):
    at = pl.program_id(0)

    @pl.when(at < cut)
    def _():
        high_ref[0], low_ref[0] = split(one_ref[0])

    @pl.when(at >= cut)
    def _():
        high_ref[0], low_ref[0] = split(two_ref[0])


def split_blocks(one, two):
    cut, rows, deep = one.shape
    count = cut + two.shape[0]
    out = jax.ShapeDtypeStruct((count, rows, deep), jnp.bfloat16)
    out_spec = pl.BlockSpec((1, rows, deep), lambda g: (g, 0, 0))
    return pl.pallas_call(
        functools.partial(split_blocks_body, cut),
        grid=(count,),
        in_specs=[
            pl.BlockSpec((1, rows, deep), lambda g: (jnp.minimum(g, cut - 1), 0, 0)),
            pl.BlockSpec((1, rows, deep), lambda g: (jnp.maximum(g - cut, 0), 0, 0)),
        ],
        out_specs=[out_spec, out_spec],
        out_shape=[out, out],
        name="split_blocks",
        compiler_params=pltpu.CompilerParams(vmem_limit_bytes=SMALL),
        cost_estimate=pl.CostEstimate(flops=0, bytes_accessed=8 * count * rows * deep, transcendentals=0),
    )(one, two)


def product_body(terms, has_start, around_ref, *refs):
    del around_ref
    out_ref = refs[-1]
    dot = functools.partial(jnp.dot, preferred_element_type=jnp.float32)
    total = refs[3 * terms][0] if has_start else None
    for t in range(terms):
        left_high, left_low, right_ref = refs[3 * t : 3 * t + 3]
        high, low = split(right_ref[0])
        part = dot(left_high[0], high) + (dot(left_high[0], low) + dot(left_low[0], high))
        total = part if total is None else total + part
    out_ref[0] = total


def products(around, a_high, a_low, panels, first, count, start=None):
    deep, cols = panels[0].shape[1:]
    rows = a_high.shape[1]
    ordered = panels[0].shape[0] == count < len(OFFSETS)

    def left_at(s):
        return lambda g, around: (around[first + g] + s, 0, 0)

    def right_at(g, around):
        return (g if ordered else around[first + g], 0, 0)

    in_specs, args = [], []
    for s, panel in enumerate(panels):
        in_specs += [pl.BlockSpec((1, rows, deep), left_at(s))] * 2
        in_specs += [pl.BlockSpec((1, deep, cols), right_at)]
        args += [a_high, a_low, panel]
    if start is not None:
        in_specs += [pl.BlockSpec((1, rows, cols), lambda g, around: (first + g, 0, 0))]
        args += [start]
    blocks = count * len(panels)
    return pl.pallas_call(
        functools.partial(product_body, len(panels), start is not None),
        grid_spec=pltpu.PrefetchScalarGridSpec(
            num_scalar_prefetch=1,
            grid=(count,),
            in_specs=in_specs,
            out_specs=pl.BlockSpec((1, rows, cols), lambda g, around: (g, 0, 0)),
        ),
        out_shape=jax.ShapeDtypeStruct((count, rows, cols), jnp.float32),
        name="products",
        compiler_params=pltpu.CompilerParams(vmem_limit_bytes=SMALL),
        cost_estimate=pl.CostEstimate(
            flops=6 * blocks * rows * deep * cols, bytes_accessed=8 * blocks * deep * cols, transcendentals=0
        ),
    )(around, *args)


def shifted(block, axes, distance):
    n = lax.axis_size(axes)
    return lax.ppermute(block, axes, [((i - distance) % n, i) for i in range(n)])


def exchange(block, axes):
    return lax.all_to_all(block, axes, split_axis=0, concat_axis=0, tiled=True)


def on_device(a_stored, b_stored):
    blocks = lax.axis_size(ROW)
    planes = lax.axis_size("z")
    deep = b_stored.shape[0] // blocks
    row_index = lax.axis_index(ROW).astype(jnp.int32)
    col_index = lax.axis_index(COL).astype(jnp.int32)
    plane = lax.axis_index("z").astype(jnp.int32)
    side = lax.axis_index("y_lo").astype(jnp.int32)
    kinds = jnp.arange(planes + WINDOW - 1, dtype=jnp.int32)
    mine = (row_index + side * planes + kinds) % blocks
    theirs = (row_index + (1 - side) * planes + kinds) % blocks
    around = (plane + jnp.array(OFFSETS, dtype=jnp.int32)) % planes
    order = (jnp.arange(blocks, dtype=jnp.int32) + col_index + 1) % blocks
    (panel,) = order_blocks(b_stored, order, deep, 0, (blocks,), "order_panel")
    panel = exchange(panel, ROW).reshape(2, planes, deep, panel.shape[2])

    one = lax.dynamic_index_in_dim(panel, side, 0, keepdims=False)
    theirs, one = lax.optimization_barrier((theirs, one))
    panel, _ = lax.optimization_barrier((panel, one))
    two = lax.dynamic_index_in_dim(panel, 1 - side, 0, keepdims=False)
    early, late = order_blocks(a_stored, theirs, deep, 1, (EARLY, planes + WINDOW - 1 - EARLY), "order_slab")
    early = shifted(early, "y_lo", 1)
    a_own = split_stored(a_stored, mine, deep)
    one = exchange(one, "z")
    two, one, early, late, *a_own = lax.optimization_barrier((two, one, early, late, *a_own))
    late = shifted(late, "y_lo", 1)
    one_before, one_after = shifted(one, ROW, 1), shifted(one, ROW, -1)
    two = exchange(two, "z")
    a_other = split_blocks(early, late)
    total = products(around, *a_own, [one_before, one, one_after], 0, planes)

    two, total, *a_other = lax.optimization_barrier((two, total, *a_other))
    groups = order_blocks(two.reshape(-1, two.shape[2]), around, deep, 0, GROUPS, "order_rest", SMALL)
    rest = [[shifted(group, ROW, 1), group, shifted(group, ROW, -1)] for group in groups]
    first, done = 0, []
    for group, count in zip(rest, GROUPS):
        done.append(products(around, *a_other, group, first, count, total))
        first += count
    far, mid, near = done
    ahead = shifted(far[0], "z", 1)
    behind = shifted(far[1], "z", -1)
    ahead = shifted(mid[0] + ahead, "z", 1)
    behind = shifted(mid[1] + behind, "z", -1)
    ahead = shifted(near[0] + ahead, "z", 1)
    behind = shifted(near[1] + behind, "z", -1)
    ahead = shifted(near[2] + ahead, "z", 1)
    return (near[3] + behind) + ahead


def solution(mesh):
    split_mesh = Mesh(np.array(mesh.devices).reshape(2, 4, 2, 2, 8), AXES)
    return jax.shard_map(
        on_device,
        mesh=split_mesh,
        in_specs=(P(ROW, COL), P(ROW, COL)),
        out_specs=P(ROW, COL),
        check_vma=False,
    )
```

```python
import functools

import jax
import jax.numpy as jnp
import numpy as np
from jax import lax
from jax.experimental import pallas as pl
from jax.experimental.pallas import tpu as pltpu
from jax.sharding import Mesh
from jax.sharding import PartitionSpec as P

AXES = ("y_hi", "x", "core", "y_lo", "z")
ROW, COL = AXES[:3], AXES[3:]
WINDOW = 3
OFFSETS = (4, -3, 3, -2, 2, -1, 1, 0)
GROUPS = (2, 2, 4)
EARLY = 2
LARGE = 60 * 2**20
SMALL = 16 * 2**20


def order_body(along, index_ref, in_ref, *refs):
    out_refs, (held, in_sems, out_sems) = refs[:-3], refs[-3:]
    count, deep = held.shape[0], held.shape[1 + along]

    def bring(d):
        span = pl.ds(pl.multiple_of(index_ref[d] * deep, deep), deep)
        part = in_ref.at[span, :] if along == 0 else in_ref.at[:, span]
        return pltpu.make_async_copy(part, held.at[d], in_sems.at[d])

    places = [(out_ref, d) for out_ref in out_refs for d in range(out_ref.shape[0])]
    puts = [pltpu.make_async_copy(held.at[d], out.at[e], out_sems.at[d]) for d, (out, e) in enumerate(places)]
    for d in range(count):
        bring(d).start()
    for d in range(count):
        bring(d).wait()
        puts[d].start()
    for put in puts:
        put.wait()


def order_blocks(stored, index, deep, along, parts, name, room=LARGE):
    count = index.shape[0]
    shape = (deep, stored.shape[1]) if along == 0 else (stored.shape[0], deep)
    return pl.pallas_call(
        functools.partial(order_body, along),
        in_specs=[pl.BlockSpec(memory_space=pltpu.SMEM), pl.BlockSpec(memory_space=pl.ANY)],
        out_specs=[pl.BlockSpec(memory_space=pl.ANY)] * len(parts),
        out_shape=[jax.ShapeDtypeStruct((part, *shape), jnp.float32) for part in parts],
        scratch_shapes=[
            pltpu.VMEM((count, *shape), jnp.float32),
            pltpu.SemaphoreType.DMA((count,)),
            pltpu.SemaphoreType.DMA((count,)),
        ],
        name=name,
        compiler_params=pltpu.CompilerParams(vmem_limit_bytes=room),
        cost_estimate=pl.CostEstimate(flops=0, bytes_accessed=8 * count * shape[0] * shape[1], transcendentals=0),
    )(index, stored)


def split(value):
    high = value.astype(jnp.bfloat16)
    low = (value - high.astype(jnp.float32)).astype(jnp.bfloat16)
    return high, low


def split_stored_body(index_ref, in_ref, high_ref, low_ref):
    del index_ref
    high_ref[0], low_ref[0] = split(in_ref[...])


def split_stored(a_stored, index, deep):
    count, rows = index.shape[0], a_stored.shape[0]
    out = jax.ShapeDtypeStruct((count, rows, deep), jnp.bfloat16)
    out_spec = pl.BlockSpec((1, rows, deep), lambda g, index: (g, 0, 0))
    return pl.pallas_call(
        split_stored_body,
        grid_spec=pltpu.PrefetchScalarGridSpec(
            num_scalar_prefetch=1,
            grid=(count,),
            in_specs=[pl.BlockSpec((rows, deep), lambda g, index: (0, index[g]))],
            out_specs=[out_spec, out_spec],
        ),
        out_shape=[out, out],
        name="split_stored",
        compiler_params=pltpu.CompilerParams(vmem_limit_bytes=LARGE),
        cost_estimate=pl.CostEstimate(flops=0, bytes_accessed=8 * count * rows * deep, transcendentals=0),
    )(index, a_stored)


def split_blocks_body(cut, one_ref, two_ref, high_ref, low_ref):
    at = pl.program_id(0)

    @pl.when(at < cut)
    def _():
        high_ref[0], low_ref[0] = split(one_ref[0])

    @pl.when(at >= cut)
    def _():
        high_ref[0], low_ref[0] = split(two_ref[0])


def split_blocks(one, two):
    cut, rows, deep = one.shape
    count = cut + two.shape[0]
    out = jax.ShapeDtypeStruct((count, rows, deep), jnp.bfloat16)
    out_spec = pl.BlockSpec((1, rows, deep), lambda g: (g, 0, 0))
    return pl.pallas_call(
        functools.partial(split_blocks_body, cut),
        grid=(count,),
        in_specs=[
            pl.BlockSpec((1, rows, deep), lambda g: (jnp.minimum(g, cut - 1), 0, 0)),
            pl.BlockSpec((1, rows, deep), lambda g: (jnp.maximum(g - cut, 0), 0, 0)),
        ],
        out_specs=[out_spec, out_spec],
        out_shape=[out, out],
        name="split_blocks",
        compiler_params=pltpu.CompilerParams(vmem_limit_bytes=SMALL),
        cost_estimate=pl.CostEstimate(flops=0, bytes_accessed=8 * count * rows * deep, transcendentals=0),
    )(one, two)


def product_body(cut, first, ordered, has_start, place_ref, *refs):
    out_ref = refs[-1]
    at = pl.program_id(0)
    at = at if ordered else place_ref[first + at]
    dot = functools.partial(jnp.dot, preferred_element_type=jnp.float32)
    own_ref, other_ref, one_ref, two_ref = refs[:4]
    rights = [own_ref[0], other_ref[0], jnp.where(at < cut, one_ref[0], two_ref[0])]
    total = refs[10][0] if has_start else None
    for t, right in enumerate(rights):
        left_high, left_low = refs[4 + 2 * t : 6 + 2 * t]
        high, low = split(right)
        part = dot(left_high[0], high) + (dot(left_high[0], low) + dot(left_low[0], high))
        total = part if total is None else total + part
    out_ref[0] = total


def products(place, a_high, a_low, panels, first, count, base=None, start=None):
    own, other, one, two = panels
    deep, cols = own.shape[1:]
    rows, cut = a_high.shape[1], one.shape[0]
    ordered = base is not None

    def left_at(term):
        return lambda g, place: (place[first + g] + place[len(OFFSETS) + term], 0, 0)

    def right_at(offset, low, high):
        def at(g, place):
            index = g + offset if ordered else place[first + g]
            return (jnp.clip(index - low, 0, high - 1), 0, 0)

        return at

    block = (1, deep, cols)
    in_specs = [
        pl.BlockSpec(block, right_at(base or 0, 0, own.shape[0])),
        pl.BlockSpec(block, right_at(base or 0, 0, other.shape[0])),
        pl.BlockSpec(block, right_at(0, 0, cut)),
        pl.BlockSpec(block, right_at(0, cut, two.shape[0])),
    ]
    for term in range(WINDOW):
        in_specs += [pl.BlockSpec((1, rows, deep), left_at(term))] * 2
    args = [own, other, one, two] + [a_high, a_low] * WINDOW
    if start is not None:
        in_specs += [pl.BlockSpec((1, rows, cols), lambda g, place: (first + g, 0, 0))]
        args += [start]
    blocks = count * WINDOW
    return pl.pallas_call(
        functools.partial(product_body, cut, first, ordered, start is not None),
        grid_spec=pltpu.PrefetchScalarGridSpec(
            num_scalar_prefetch=1,
            grid=(count,),
            in_specs=in_specs,
            out_specs=pl.BlockSpec((1, rows, cols), lambda g, place: (g, 0, 0)),
        ),
        out_shape=jax.ShapeDtypeStruct((count, rows, cols), jnp.float32),
        name="products",
        compiler_params=pltpu.CompilerParams(vmem_limit_bytes=SMALL),
        cost_estimate=pl.CostEstimate(
            flops=6 * blocks * rows * deep * cols, bytes_accessed=8 * blocks * deep * cols, transcendentals=0
        ),
    )(place, *args)


def shifted(block, axes, distance):
    n = lax.axis_size(axes)
    return lax.ppermute(block, axes, [((i - distance) % n, i) for i in range(n)])


def to_other_core(block):
    return lax.ppermute(block, ROW, [(i, i ^ 1) for i in range(lax.axis_size(ROW))])


def to_next_chips(own, other):
    n = lax.axis_size(ROW)
    one = lax.ppermute(own, ROW, [(i, (i + (1 if i % 2 else -1)) % n) for i in range(n)])
    two = lax.ppermute(other, ROW, [(i, (i + (-2 if i % 2 else 2)) % n) for i in range(n)])
    return one, two


def exchange(block, axes):
    return lax.all_to_all(block, axes, split_axis=0, concat_axis=0, tiled=True)


def on_device(a_stored, b_stored):
    blocks = lax.axis_size(ROW)
    planes = lax.axis_size("z")
    deep = b_stored.shape[0] // blocks
    row_index = lax.axis_index(ROW).astype(jnp.int32)
    col_index = lax.axis_index(COL).astype(jnp.int32)
    plane = lax.axis_index("z").astype(jnp.int32)
    side = lax.axis_index("y_lo").astype(jnp.int32)
    kinds = jnp.arange(planes + WINDOW - 1, dtype=jnp.int32)
    mine = (row_index + side * planes + kinds) % blocks
    theirs = (row_index + (1 - side) * planes + kinds) % blocks
    around = (plane + jnp.array(OFFSETS, dtype=jnp.int32)) % planes
    core = lax.axis_index("core").astype(jnp.int32)
    place = jnp.concatenate([around, jnp.stack([jnp.ones_like(core), 2 - 2 * core, 2 * core])])
    order = (jnp.arange(blocks, dtype=jnp.int32) + col_index + 1) % blocks
    (panel,) = order_blocks(b_stored, order, deep, 0, (blocks,), "order_panel")
    theirs, panel = lax.optimization_barrier((theirs, panel))
    early, late = order_blocks(a_stored, theirs, deep, 1, (EARLY, planes + WINDOW - 1 - EARLY), "order_slab")
    early = shifted(early, "y_lo", 1)
    panel = exchange(panel, ROW)
    panel, early, late = lax.optimization_barrier((panel, early, late))
    panel = panel.reshape(2, planes, deep, panel.shape[2])

    one = lax.dynamic_index_in_dim(panel, side, 0, keepdims=False)
    late, mine, one = lax.optimization_barrier((late, mine, one))
    panel, _ = lax.optimization_barrier((panel, one))
    two = lax.dynamic_index_in_dim(panel, 1 - side, 0, keepdims=False)
    late = shifted(late, "y_lo", 1)
    a_own = split_stored(a_stored, mine, deep)
    one = exchange(one, "z")
    two, one, late, *a_own = lax.optimization_barrier((two, one, late, *a_own))
    one_other = to_other_core(one)
    one_next = to_next_chips(one[: planes // 2], one_other[planes // 2 :])
    two = exchange(two, "z")
    a_other = split_blocks(early, late)
    total = products(place, *a_own, [one, one_other, *one_next], 0, planes)

    two, total, *a_other = lax.optimization_barrier((two, total, *a_other))
    groups = order_blocks(two.reshape(-1, two.shape[2]), around, deep, 0, GROUPS, "order_rest", SMALL)
    others = [to_other_core(group) for group in groups]
    done, first = [], 0
    for own, other, count in zip(groups, others, GROUPS):
        came = to_next_chips(own[: count // 2], other[count // 2 :])
        part = products(place, *a_other, [own, other, *came], first, count, 0, total)
        done += [part[g] for g in range(count)]
        first += count
    ahead, behind = shifted(done[0], "z", 1), shifted(done[1], "z", -1)
    for far in (2, 4):
        ahead = shifted(done[far] + ahead, "z", 1)
        behind = shifted(done[far + 1] + behind, "z", -1)
    ahead = shifted(done[6] + ahead, "z", 1)
    return (done[7] + behind) + ahead


def solution(mesh):
    split_mesh = Mesh(np.array(mesh.devices).reshape(2, 4, 2, 2, 8), AXES)
    return jax.shard_map(
        on_device,
        mesh=split_mesh,
        in_specs=(P(ROW, COL), P(ROW, COL)),
        out_specs=P(ROW, COL),
        check_vma=False,
    )
```

```python
import functools

import jax
import jax.numpy as jnp
import numpy as np
from jax import lax
from jax.experimental import pallas as pl
from jax.experimental.pallas import tpu as pltpu
from jax.sharding import Mesh
from jax.sharding import PartitionSpec as P

AXES = ("y_hi", "x", "core", "y_lo", "z")
ROW, COL = AXES[:3], AXES[3:]
WINDOW = 3
OFFSETS = (4, -3, 3, -2, 2, -1, 1, 0)
GROUPS = (2, 2, 4)
EARLY = 3
LATE = 5
LARGE = 60 * 2**20
SMALL = 16 * 2**20


def order_body(along, index_ref, in_ref, *refs):
    out_refs, (held, in_sems, out_sems) = refs[:-3], refs[-3:]
    count, deep = held.shape[0], held.shape[1 + along]

    def bring(d):
        span = pl.ds(pl.multiple_of(index_ref[d] * deep, deep), deep)
        part = in_ref.at[span, :] if along == 0 else in_ref.at[:, span]
        return pltpu.make_async_copy(part, held.at[d], in_sems.at[d])

    places = [(out_ref, d) for out_ref in out_refs for d in range(out_ref.shape[0])]
    puts = [pltpu.make_async_copy(held.at[d], out.at[e], out_sems.at[d]) for d, (out, e) in enumerate(places)]
    for d in range(count):
        bring(d).start()
    for d in range(count):
        bring(d).wait()
        puts[d].start()
    for put in puts:
        put.wait()


def order_blocks(stored, index, deep, along, parts, name, room=LARGE):
    count = index.shape[0]
    shape = (deep, stored.shape[1]) if along == 0 else (stored.shape[0], deep)
    return pl.pallas_call(
        functools.partial(order_body, along),
        in_specs=[pl.BlockSpec(memory_space=pltpu.SMEM), pl.BlockSpec(memory_space=pl.ANY)],
        out_specs=[pl.BlockSpec(memory_space=pl.ANY)] * len(parts),
        out_shape=[jax.ShapeDtypeStruct((part, *shape), jnp.float32) for part in parts],
        scratch_shapes=[
            pltpu.VMEM((count, *shape), jnp.float32),
            pltpu.SemaphoreType.DMA((count,)),
            pltpu.SemaphoreType.DMA((count,)),
        ],
        name=name,
        compiler_params=pltpu.CompilerParams(vmem_limit_bytes=room),
        cost_estimate=pl.CostEstimate(flops=0, bytes_accessed=8 * count * shape[0] * shape[1], transcendentals=0),
    )(index, stored)


def split(value):
    high = value.astype(jnp.bfloat16)
    low = (value - high.astype(jnp.float32)).astype(jnp.bfloat16)
    return high, low


def move_body(sources, index_ref, *refs):
    count = len(sources)
    held, in_sems, out_sems = refs[-3:]
    inputs = max(which for which, _ in sources) + 1
    in_refs, out_refs = refs[:inputs], refs[inputs:-3]
    if len(out_refs) == 1:
        places = [(out_refs[0], index_ref[d]) for d in range(count)]
    else:
        places = [(out_ref, d) for out_ref in out_refs for d in range(out_ref.shape[0])]
    brings = [
        pltpu.make_async_copy(in_refs[which].at[e], held.at[d], in_sems.at[d])
        for d, (which, e) in enumerate(sources)
    ]
    puts = [pltpu.make_async_copy(held.at[d], out.at[e], out_sems.at[d]) for d, (out, e) in enumerate(places)]
    for bring in brings:
        bring.start()
    for bring, put in zip(brings, puts):
        bring.wait()
        put.start()
    for put in puts:
        put.wait()


def move_blocks(inputs, sources, parts, index, name):
    shape, count = inputs[0].shape[1:], len(sources)
    return pl.pallas_call(
        functools.partial(move_body, sources),
        in_specs=[pl.BlockSpec(memory_space=pltpu.SMEM)] + [pl.BlockSpec(memory_space=pl.ANY)] * len(inputs),
        out_specs=[pl.BlockSpec(memory_space=pl.ANY)] * len(parts),
        out_shape=[jax.ShapeDtypeStruct((part, *shape), jnp.float32) for part in parts],
        scratch_shapes=[
            pltpu.VMEM((count, *shape), jnp.float32),
            pltpu.SemaphoreType.DMA((count,)),
            pltpu.SemaphoreType.DMA((count,)),
        ],
        name=name,
        compiler_params=pltpu.CompilerParams(vmem_limit_bytes=LARGE),
        cost_estimate=pl.CostEstimate(flops=0, bytes_accessed=8 * count * shape[0] * shape[1], transcendentals=0),
    )(index, *inputs)


def split_body(cut, index_ref, own_ref, one_ref, two_ref, high_ref, low_ref):
    del index_ref
    deep = own_ref.shape[1]
    high_ref[0, :, :deep], low_ref[0, :, :deep] = split(own_ref[...])
    other = jnp.where(pl.program_id(0) < cut, one_ref[0], two_ref[0])
    high_ref[0, :, deep:], low_ref[0, :, deep:] = split(other)


def split_slab(a_stored, index, one, two):
    cut, rows, deep = one.shape
    count = cut + two.shape[0]
    out = jax.ShapeDtypeStruct((count, rows, 2 * deep), jnp.bfloat16)
    out_spec = pl.BlockSpec((1, rows, 2 * deep), lambda g, index: (g, 0, 0))
    return pl.pallas_call(
        functools.partial(split_body, cut),
        grid_spec=pltpu.PrefetchScalarGridSpec(
            num_scalar_prefetch=1,
            grid=(count,),
            in_specs=[
                pl.BlockSpec((rows, deep), lambda g, index: (0, index[g])),
                pl.BlockSpec((1, rows, deep), lambda g, index: (jnp.minimum(g, cut - 1), 0, 0)),
                pl.BlockSpec((1, rows, deep), lambda g, index: (jnp.maximum(g - cut, 0), 0, 0)),
            ],
            out_specs=[out_spec, out_spec],
        ),
        out_shape=[out, out],
        name="split_slab",
        compiler_params=pltpu.CompilerParams(vmem_limit_bytes=SMALL),
        cost_estimate=pl.CostEstimate(flops=0, bytes_accessed=16 * count * rows * deep, transcendentals=0),
    )(index, a_stored, one, two)


def product_body(cut, first, ordered, has_start, place_ref, *refs):
    out_ref = refs[-1]
    at = pl.program_id(0)
    at = at if ordered else place_ref[first + at]
    dot = functools.partial(jnp.dot, preferred_element_type=jnp.float32)
    own_ref, other_ref, one_ref, two_ref = refs[:4]
    rights = [own_ref[0], other_ref[0], jnp.where(at < cut, one_ref[0], two_ref[0])]
    total = refs[10][0] if has_start else None
    for t, right in enumerate(rights):
        left_high, left_low = refs[4 + 2 * t : 6 + 2 * t]
        high, low = split(right)
        part = dot(left_high[0], high) + (dot(left_high[0], low) + dot(left_low[0], high))
        total = part if total is None else total + part
    out_ref[0] = total


def products(place, a_high, a_low, panels, first, count, base=None, start=None):
    own, other, one, two = panels
    deep, cols = own.shape[1:]
    rows, cut = a_high.shape[1], one.shape[0]
    ordered = base is not None

    def left_at(term):
        return lambda g, place: (place[first + g] + place[len(OFFSETS) + term], 0, 0)

    def right_at(offset, low, high):
        def at(g, place):
            index = g + offset if ordered else place[first + g]
            return (jnp.clip(index - low, 0, high - 1), 0, 0)

        return at

    block = (1, deep, cols)
    in_specs = [
        pl.BlockSpec(block, right_at(base or 0, 0, own.shape[0])),
        pl.BlockSpec(block, right_at(base or 0, 0, other.shape[0])),
        pl.BlockSpec(block, right_at(0, 0, cut)),
        pl.BlockSpec(block, right_at(0, cut, two.shape[0])),
    ]
    for term in range(WINDOW):
        in_specs += [pl.BlockSpec((1, rows, deep), left_at(term))] * 2
    args = [own, other, one, two] + [a_high, a_low] * WINDOW
    if start is not None:
        in_specs += [pl.BlockSpec((1, rows, cols), lambda g, place: (first + g, 0, 0))]
        args += [start]
    blocks = count * WINDOW
    return pl.pallas_call(
        functools.partial(product_body, cut, first, ordered, start is not None),
        grid_spec=pltpu.PrefetchScalarGridSpec(
            num_scalar_prefetch=1,
            grid=(count,),
            in_specs=in_specs,
            out_specs=pl.BlockSpec((1, rows, cols), lambda g, place: (g, 0, 0)),
        ),
        out_shape=jax.ShapeDtypeStruct((count, rows, cols), jnp.float32),
        name="products",
        compiler_params=pltpu.CompilerParams(vmem_limit_bytes=SMALL),
        cost_estimate=pl.CostEstimate(
            flops=6 * blocks * rows * deep * cols, bytes_accessed=8 * blocks * deep * cols, transcendentals=0
        ),
    )(place, *args)


def shifted(block, axes, distance):
    n = lax.axis_size(axes)
    return lax.ppermute(block, axes, [((i - distance) % n, i) for i in range(n)])


def to_other_core(block):
    return lax.ppermute(block, ROW, [(i, i ^ 1) for i in range(lax.axis_size(ROW))])


def to_next_chips(own, other):
    n = lax.axis_size(ROW)
    one = lax.ppermute(own, ROW, [(i, (i + (1 if i % 2 else -1)) % n) for i in range(n)])
    two = lax.ppermute(other, ROW, [(i, (i + (-2 if i % 2 else 2)) % n) for i in range(n)])
    return one, two


def exchange(block, axes):
    return lax.all_to_all(block, axes, split_axis=0, concat_axis=0, tiled=True)


def on_device(a_stored, b_stored):
    blocks = lax.axis_size(ROW)
    planes = lax.axis_size("z")
    deep = b_stored.shape[0] // blocks
    row_index = lax.axis_index(ROW).astype(jnp.int32)
    col_index = lax.axis_index(COL).astype(jnp.int32)
    plane = lax.axis_index("z").astype(jnp.int32)
    side = lax.axis_index("y_lo").astype(jnp.int32)
    kinds = jnp.arange(planes + WINDOW - 1, dtype=jnp.int32)
    mine = (row_index + side * planes + kinds) % blocks
    theirs = (row_index + (1 - side) * planes + kinds) % blocks
    around = (plane + jnp.array(OFFSETS, dtype=jnp.int32)) % planes
    core = lax.axis_index("core").astype(jnp.int32)
    place = jnp.concatenate([around, jnp.stack([jnp.ones_like(core), 2 - 2 * core, 2 * core])])
    half = deep // 2
    y_hi, x = lax.axis_index("y_hi").astype(jnp.int32), lax.axis_index("x").astype(jnp.int32)
    x_count = lax.axis_size("x")

    order = (jnp.arange(blocks, dtype=jnp.int32) + col_index + 1) % blocks
    (panel,) = order_blocks(b_stored, 2 * order, half, 0, (blocks,), "order_panel")

    step = jnp.arange(blocks, dtype=jnp.int32)
    to_core, to_y, to_x = step // (2 * x_count) ^ core, step // x_count % 2 ^ y_hi, (step % x_count + x) % x_count
    far = (to_y * planes + to_x * 2 + to_core + col_index + 1) % blocks
    far, panel = lax.optimization_barrier((far, panel))
    here, there = order_blocks(b_stored, 2 * far + 1, half, 0, (planes, planes), "order_panel")
    there = to_other_core(there)
    slab = jnp.concatenate([2 * theirs, 2 * theirs + 1])
    slab, panel = lax.optimization_barrier((slab, panel))
    kinds = kinds.shape[0]
    slabs = list(order_blocks(a_stored, slab, half, 1, (EARLY, kinds - EARLY, LATE, kinds - LATE), "order_slab"))
    here_across = shifted(here[x_count:], "y_hi", 1)
    panel = exchange(panel, ROW)
    slabs[0] = shifted(slabs[0], "y_lo", 1)
    panel, here_across, *slabs = lax.optimization_barrier((panel, here_across, *slabs))

    pieces = (step % 2 ^ side) * planes + step // 2
    (one,) = order_blocks(panel.reshape(-1, panel.shape[2]), pieces, half, 0, (blocks,), "order_planes")
    there, one = lax.optimization_barrier((there, one))
    there_across = shifted(there[x_count:], "y_hi", 1)
    there_across, *slabs = lax.optimization_barrier((there_across, *slabs))
    slabs[1:3] = [shifted(slab, "y_lo", 1) for slab in slabs[1:3]]
    held = [here, here_across, there, there_across]
    sources = tuple((which, distance) for distance in range(x_count) for which in range(4))
    along = move_blocks(held, sources, (4,) * x_count, step, "order_distance")
    along = [along[0]] + [shifted(along[d], "x", d) for d in range(1, x_count)]
    from_x, from_core, from_y = (x - step // 4) % x_count, step // 2 % 2 ^ core, step % 2 ^ y_hi
    goal = (from_x * 2 + from_core) * 2 + (from_y ^ side)
    sources = tuple((distance, e) for distance in range(x_count) for e in range(4))
    (two,) = move_blocks(along, sources, (blocks,), goal, "order_planes")
    one, two = one.reshape(planes, deep, -1), two.reshape(planes, deep, -1)

    one = exchange(one, "z")
    two, one, *slabs = lax.optimization_barrier((two, one, *slabs))
    slabs[3] = shifted(slabs[3], "y_lo", 1)
    one_other = to_other_core(one)
    one_next = to_next_chips(one[: planes // 2], one_other[planes // 2 :])
    two = exchange(two, "z")
    a_first = split_slab(a_stored, 2 * mine, *slabs[:2])
    total = products(place, *a_first, [one, one_other, *one_next], 0, planes)
    total, *slabs = lax.optimization_barrier((total, *slabs))
    a_second = split_slab(a_stored, 2 * mine + 1, *slabs[2:])

    two, total, *a_second = lax.optimization_barrier((two, total, *a_second))
    groups = order_blocks(two.reshape(-1, two.shape[2]), around, deep, 0, GROUPS, "order_rest", SMALL)
    others = [to_other_core(group) for group in groups]
    done, first = [], 0
    for own, other, count in zip(groups, others, GROUPS):
        came = to_next_chips(own[: count // 2], other[count // 2 :])
        part = products(place, *a_second, [own, other, *came], first, count, 0, total)
        done += [part[g] for g in range(count)]
        first += count
    ahead, behind = shifted(done[0], "z", 1), shifted(done[1], "z", -1)
    for far in (2, 4):
        ahead = shifted(done[far] + ahead, "z", 1)
        behind = shifted(done[far + 1] + behind, "z", -1)
    ahead = shifted(done[6] + ahead, "z", 1)
    return (done[7] + behind) + ahead


def solution(mesh):
    split_mesh = Mesh(np.array(mesh.devices).reshape(2, 4, 2, 2, 8), AXES)
    return jax.shard_map(
        on_device,
        mesh=split_mesh,
        in_specs=(P(ROW, COL), P(ROW, COL)),
        out_specs=P(ROW, COL),
        check_vma=False,
    )
```

```python
import functools

import jax
import jax.numpy as jnp
import numpy as np
from jax import lax
from jax.experimental import pallas as pl
from jax.experimental.pallas import tpu as pltpu
from jax.sharding import Mesh
from jax.sharding import PartitionSpec as P

AXES = ("y_hi", "x", "core", "y_lo", "z")
ROW, COL = AXES[:3], AXES[3:]
WINDOW = 3
OFFSETS = (4, -3, 3, -2, 2, -1, 1, 0)
GROUPS = (2, 2, 2, 2)
EARLY = 3
LATE = 5
LARGE = 60 * 2**20
SMALL = 16 * 2**20


def order_body(along, index_ref, in_ref, *refs):
    out_refs, (held, in_sems, out_sems) = refs[:-3], refs[-3:]
    count, deep = held.shape[0], held.shape[1 + along]

    def bring(d):
        span = pl.ds(pl.multiple_of(index_ref[d] * deep, deep), deep)
        part = in_ref.at[span, :] if along == 0 else in_ref.at[:, span]
        return pltpu.make_async_copy(part, held.at[d], in_sems.at[d])

    places = [(out_ref, d) for out_ref in out_refs for d in range(out_ref.shape[0])]
    puts = [pltpu.make_async_copy(held.at[d], out.at[e], out_sems.at[d]) for d, (out, e) in enumerate(places)]
    for d in range(count):
        bring(d).start()
    for d in range(count):
        bring(d).wait()
        puts[d].start()
    for put in puts:
        put.wait()


def order_blocks(stored, index, deep, along, parts, name, room=LARGE):
    count = index.shape[0]
    shape = (deep, stored.shape[1]) if along == 0 else (stored.shape[0], deep)
    return pl.pallas_call(
        functools.partial(order_body, along),
        in_specs=[pl.BlockSpec(memory_space=pltpu.SMEM), pl.BlockSpec(memory_space=pl.ANY)],
        out_specs=[pl.BlockSpec(memory_space=pl.ANY)] * len(parts),
        out_shape=[jax.ShapeDtypeStruct((part, *shape), jnp.float32) for part in parts],
        scratch_shapes=[
            pltpu.VMEM((count, *shape), jnp.float32),
            pltpu.SemaphoreType.DMA((count,)),
            pltpu.SemaphoreType.DMA((count,)),
        ],
        name=name,
        compiler_params=pltpu.CompilerParams(vmem_limit_bytes=room),
        cost_estimate=pl.CostEstimate(flops=0, bytes_accessed=8 * count * shape[0] * shape[1], transcendentals=0),
    )(index, stored)


def split(value):
    high = value.astype(jnp.bfloat16)
    low = (value - high.astype(jnp.float32)).astype(jnp.bfloat16)
    return high, low


def move_body(sources, index_ref, *refs):
    count = len(sources)
    held, in_sems, out_sems = refs[-3:]
    inputs = max(which for which, _ in sources) + 1
    in_refs, out_refs = refs[:inputs], refs[inputs:-3]
    if len(out_refs) == 1:
        places = [(out_refs[0], index_ref[d]) for d in range(count)]
    else:
        places = [(out_ref, d) for out_ref in out_refs for d in range(out_ref.shape[0])]
    brings = [
        pltpu.make_async_copy(in_refs[which].at[e], held.at[d], in_sems.at[d])
        for d, (which, e) in enumerate(sources)
    ]
    puts = [pltpu.make_async_copy(held.at[d], out.at[e], out_sems.at[d]) for d, (out, e) in enumerate(places)]
    for bring in brings:
        bring.start()
    for bring, put in zip(brings, puts):
        bring.wait()
        put.start()
    for put in puts:
        put.wait()


def move_blocks(inputs, sources, parts, index, name):
    shape, count = inputs[0].shape[1:], len(sources)
    return pl.pallas_call(
        functools.partial(move_body, sources),
        in_specs=[pl.BlockSpec(memory_space=pltpu.SMEM)] + [pl.BlockSpec(memory_space=pl.ANY)] * len(inputs),
        out_specs=[pl.BlockSpec(memory_space=pl.ANY)] * len(parts),
        out_shape=[jax.ShapeDtypeStruct((part, *shape), jnp.float32) for part in parts],
        scratch_shapes=[
            pltpu.VMEM((count, *shape), jnp.float32),
            pltpu.SemaphoreType.DMA((count,)),
            pltpu.SemaphoreType.DMA((count,)),
        ],
        name=name,
        compiler_params=pltpu.CompilerParams(vmem_limit_bytes=LARGE),
        cost_estimate=pl.CostEstimate(flops=0, bytes_accessed=8 * count * shape[0] * shape[1], transcendentals=0),
    )(index, *inputs)


def split_body(cut, index_ref, own_ref, one_ref, two_ref, high_ref, low_ref):
    del index_ref
    deep = own_ref.shape[1]
    high_ref[0, :, :deep], low_ref[0, :, :deep] = split(own_ref[...])
    other = jnp.where(pl.program_id(0) < cut, one_ref[0], two_ref[0])
    high_ref[0, :, deep:], low_ref[0, :, deep:] = split(other)


def split_slab(a_stored, index, one, two):
    cut, rows, deep = one.shape
    count = cut + two.shape[0]
    out = jax.ShapeDtypeStruct((count, rows, 2 * deep), jnp.bfloat16)
    out_spec = pl.BlockSpec((1, rows, 2 * deep), lambda g, index: (g, 0, 0))
    return pl.pallas_call(
        functools.partial(split_body, cut),
        grid_spec=pltpu.PrefetchScalarGridSpec(
            num_scalar_prefetch=1,
            grid=(count,),
            in_specs=[
                pl.BlockSpec((rows, deep), lambda g, index: (0, index[g])),
                pl.BlockSpec((1, rows, deep), lambda g, index: (jnp.minimum(g, cut - 1), 0, 0)),
                pl.BlockSpec((1, rows, deep), lambda g, index: (jnp.maximum(g - cut, 0), 0, 0)),
            ],
            out_specs=[out_spec, out_spec],
        ),
        out_shape=[out, out],
        name="split_slab",
        compiler_params=pltpu.CompilerParams(vmem_limit_bytes=SMALL),
        cost_estimate=pl.CostEstimate(flops=0, bytes_accessed=16 * count * rows * deep, transcendentals=0),
    )(index, a_stored, one, two)


def product_body(cut, first, ordered, has_start, place_ref, *refs):
    out_ref = refs[-1]
    at = pl.program_id(0)
    at = at if ordered else place_ref[first + at]
    dot = functools.partial(jnp.dot, preferred_element_type=jnp.float32)
    own_ref, other_ref, one_ref, two_ref = refs[:4]
    rights = [own_ref[0], other_ref[0], jnp.where(at < cut, one_ref[0], two_ref[0])]
    total = refs[10][0] if has_start else None
    for t, right in enumerate(rights):
        left_high, left_low = refs[4 + 2 * t : 6 + 2 * t]
        high, low = split(right)
        part = dot(left_high[0], high) + (dot(left_high[0], low) + dot(left_low[0], high))
        total = part if total is None else total + part
    out_ref[0] = total


def products(place, a_high, a_low, panels, first, count, base=None, start=None):
    own, other, one, two = panels
    deep, cols = own.shape[1:]
    rows, cut = a_high.shape[1], one.shape[0]
    ordered = base is not None

    def left_at(term):
        return lambda g, place: (place[first + g] + place[len(OFFSETS) + term], 0, 0)

    def right_at(offset, low, high):
        def at(g, place):
            index = g + offset if ordered else place[first + g]
            return (jnp.clip(index - low, 0, high - 1), 0, 0)

        return at

    block = (1, deep, cols)
    in_specs = [
        pl.BlockSpec(block, right_at(base or 0, 0, own.shape[0])),
        pl.BlockSpec(block, right_at(base or 0, 0, other.shape[0])),
        pl.BlockSpec(block, right_at(0, 0, cut)),
        pl.BlockSpec(block, right_at(0, cut, two.shape[0])),
    ]
    for term in range(WINDOW):
        in_specs += [pl.BlockSpec((1, rows, deep), left_at(term))] * 2
    args = [own, other, one, two] + [a_high, a_low] * WINDOW
    if start is not None:
        in_specs += [pl.BlockSpec((1, rows, cols), lambda g, place: (first + g, 0, 0))]
        args += [start]
    blocks = count * WINDOW
    return pl.pallas_call(
        functools.partial(product_body, cut, first, ordered, start is not None),
        grid_spec=pltpu.PrefetchScalarGridSpec(
            num_scalar_prefetch=1,
            grid=(count,),
            in_specs=in_specs,
            out_specs=pl.BlockSpec((1, rows, cols), lambda g, place: (g, 0, 0)),
        ),
        out_shape=jax.ShapeDtypeStruct((count, rows, cols), jnp.float32),
        name="products",
        compiler_params=pltpu.CompilerParams(vmem_limit_bytes=SMALL),
        cost_estimate=pl.CostEstimate(
            flops=6 * blocks * rows * deep * cols, bytes_accessed=8 * blocks * deep * cols, transcendentals=0
        ),
    )(place, *args)


def shifted(block, axes, distance):
    n = lax.axis_size(axes)
    return lax.ppermute(block, axes, [((i - distance) % n, i) for i in range(n)])


def to_other_core(block):
    return lax.ppermute(block, ROW, [(i, i ^ 1) for i in range(lax.axis_size(ROW))])


def to_next_chips(own, other):
    n = lax.axis_size(ROW)
    one = lax.ppermute(own, ROW, [(i, (i + (1 if i % 2 else -1)) % n) for i in range(n)])
    two = lax.ppermute(other, ROW, [(i, (i + (-2 if i % 2 else 2)) % n) for i in range(n)])
    return one, two


def exchange(block, axes):
    return lax.all_to_all(block, axes, split_axis=0, concat_axis=0, tiled=True)


def on_device(a_stored, b_stored):
    blocks = lax.axis_size(ROW)
    planes = lax.axis_size("z")
    deep = b_stored.shape[0] // blocks
    row_index = lax.axis_index(ROW).astype(jnp.int32)
    col_index = lax.axis_index(COL).astype(jnp.int32)
    plane = lax.axis_index("z").astype(jnp.int32)
    side = lax.axis_index("y_lo").astype(jnp.int32)
    kinds = jnp.arange(planes + WINDOW - 1, dtype=jnp.int32)
    mine = (row_index + side * planes + kinds) % blocks
    theirs = (row_index + (1 - side) * planes + kinds) % blocks
    around = (plane + jnp.array(OFFSETS, dtype=jnp.int32)) % planes
    core = lax.axis_index("core").astype(jnp.int32)
    place = jnp.concatenate([around, jnp.stack([jnp.ones_like(core), 2 - 2 * core, 2 * core])])
    half = deep // 2
    y_hi, x = lax.axis_index("y_hi").astype(jnp.int32), lax.axis_index("x").astype(jnp.int32)
    x_count = lax.axis_size("x")

    order = (jnp.arange(blocks, dtype=jnp.int32) + col_index + 1) % blocks
    (panel,) = order_blocks(b_stored, 2 * order, half, 0, (blocks,), "order_panel")

    step = jnp.arange(blocks, dtype=jnp.int32)
    to_core, to_y, to_x = step // (2 * x_count) ^ core, step // x_count % 2 ^ y_hi, (step % x_count + x) % x_count
    far = (to_y * planes + to_x * 2 + to_core + col_index + 1) % blocks
    far, panel = lax.optimization_barrier((far, panel))
    here, there = order_blocks(b_stored, 2 * far + 1, half, 0, (planes, planes), "order_panel")
    there = to_other_core(there)
    slab = jnp.concatenate([2 * theirs, 2 * theirs + 1])
    slab, panel = lax.optimization_barrier((slab, panel))
    kinds = kinds.shape[0]
    slabs = list(order_blocks(a_stored, slab, half, 1, (EARLY, kinds - EARLY, LATE, kinds - LATE), "order_slab"))
    here_across = shifted(here[x_count:], "y_hi", 1)
    panel = exchange(panel, ROW)
    slabs[0] = shifted(slabs[0], "y_lo", 1)
    panel, here_across, *slabs = lax.optimization_barrier((panel, here_across, *slabs))

    pieces = (step % 2 ^ side) * planes + step // 2
    (one,) = order_blocks(panel.reshape(-1, panel.shape[2]), pieces, half, 0, (blocks,), "order_planes")
    there, one = lax.optimization_barrier((there, one))
    there_across = shifted(there[x_count:], "y_hi", 1)
    there_across, *slabs = lax.optimization_barrier((there_across, *slabs))
    slabs[1:3] = [shifted(slab, "y_lo", 1) for slab in slabs[1:3]]
    held = [here, here_across, there, there_across]
    sources = tuple((which, distance) for distance in range(x_count) for which in range(4))
    along = move_blocks(held, sources, (4,) * x_count, step, "order_distance")
    along = [along[0]] + [shifted(along[d], "x", d) for d in range(1, x_count)]
    from_x, from_core, from_y = (x - step // 4) % x_count, step // 2 % 2 ^ core, step % 2 ^ y_hi
    goal = (from_x * 2 + from_core) * 2 + (from_y ^ side)
    sources = tuple((distance, e) for distance in range(x_count) for e in range(4))
    (two,) = move_blocks(along, sources, (blocks,), goal, "order_planes")
    one, two = one.reshape(planes, deep, -1), two.reshape(planes, deep, -1)

    one = exchange(one, "z")
    two, one, *slabs = lax.optimization_barrier((two, one, *slabs))
    slabs[3] = shifted(slabs[3], "y_lo", 1)
    one_other = to_other_core(one)
    one_next = to_next_chips(one[: planes // 2], one_other[planes // 2 :])
    two = exchange(two, "z")
    a_first = split_slab(a_stored, 2 * mine, *slabs[:2])
    total = products(place, *a_first, [one, one_other, *one_next], 0, planes)
    total, *slabs = lax.optimization_barrier((total, *slabs))
    a_second = split_slab(a_stored, 2 * mine + 1, *slabs[2:])

    two, total, *a_second = lax.optimization_barrier((two, total, *a_second))
    groups = order_blocks(two.reshape(-1, two.shape[2]), around, deep, 0, GROUPS, "order_rest", SMALL)
    others = [to_other_core(group) for group in groups]
    done, first = [], 0
    for own, other, count in zip(groups, others, GROUPS):
        came = to_next_chips(own[: count // 2], other[count // 2 :])
        part = products(place, *a_second, [own, other, *came], first, count, 0, total)
        done += [part[g] for g in range(count)]
        first += count
    ahead, behind = shifted(done[0], "z", 1), shifted(done[1], "z", -1)
    for far in (2, 4):
        ahead = shifted(done[far] + ahead, "z", 1)
        behind = shifted(done[far + 1] + behind, "z", -1)
    ahead = shifted(done[6] + ahead, "z", 1)
    return (done[7] + behind) + ahead


def solution(mesh):
    split_mesh = Mesh(np.array(mesh.devices).reshape(2, 4, 2, 2, 8), AXES)
    return jax.shard_map(
        on_device,
        mesh=split_mesh,
        in_specs=(P(ROW, COL), P(ROW, COL)),
        out_specs=P(ROW, COL),
        check_vma=False,
    )
```

```python
import functools

import jax
import jax.numpy as jnp
import numpy as np
from jax import lax
from jax.experimental import pallas as pl
from jax.experimental.pallas import tpu as pltpu
from jax.sharding import Mesh
from jax.sharding import PartitionSpec as P

AXES = ("y_hi", "x", "core", "y_lo", "z")
ROW, COL = AXES[:3], AXES[3:]
WINDOW = 3
OFFSETS = (4, -3, 3, -2, 2, -1, 1, 0)
GROUPS = (2, 2, 2, 2)
EARLY = 2
LATE = 5
LARGE = 60 * 2**20
SMALL = 16 * 2**20


def order_body(along, index_ref, in_ref, *refs):
    out_refs, (held, in_sems, out_sems) = refs[:-3], refs[-3:]
    count, deep = held.shape[0], held.shape[1 + along]

    def bring(d):
        span = pl.ds(pl.multiple_of(index_ref[d] * deep, deep), deep)
        part = in_ref.at[span, :] if along == 0 else in_ref.at[:, span]
        return pltpu.make_async_copy(part, held.at[d], in_sems.at[d])

    places = [(out_ref, d) for out_ref in out_refs for d in range(out_ref.shape[0])]
    puts = [pltpu.make_async_copy(held.at[d], out.at[e], out_sems.at[d]) for d, (out, e) in enumerate(places)]
    for d in range(count):
        bring(d).start()
    for d in range(count):
        bring(d).wait()
        puts[d].start()
    for put in puts:
        put.wait()


def order_blocks(stored, index, deep, along, parts, name, room=LARGE):
    count = index.shape[0]
    shape = (deep, stored.shape[1]) if along == 0 else (stored.shape[0], deep)
    return pl.pallas_call(
        functools.partial(order_body, along),
        in_specs=[pl.BlockSpec(memory_space=pltpu.SMEM), pl.BlockSpec(memory_space=pl.ANY)],
        out_specs=[pl.BlockSpec(memory_space=pl.ANY)] * len(parts),
        out_shape=[jax.ShapeDtypeStruct((part, *shape), jnp.float32) for part in parts],
        scratch_shapes=[
            pltpu.VMEM((count, *shape), jnp.float32),
            pltpu.SemaphoreType.DMA((count,)),
            pltpu.SemaphoreType.DMA((count,)),
        ],
        name=name,
        compiler_params=pltpu.CompilerParams(vmem_limit_bytes=room),
        cost_estimate=pl.CostEstimate(flops=0, bytes_accessed=8 * count * shape[0] * shape[1], transcendentals=0),
    )(index, stored)


def split(value):
    high = value.astype(jnp.bfloat16)
    low = (value - high.astype(jnp.float32)).astype(jnp.bfloat16)
    return high, low


def move_body(sources, index_ref, *refs):
    count = len(sources)
    held, in_sems, out_sems = refs[-3:]
    inputs = max(which for which, _ in sources) + 1
    in_refs, out_refs = refs[:inputs], refs[inputs:-3]
    if len(out_refs) == 1:
        places = [(out_refs[0], index_ref[d]) for d in range(count)]
    else:
        places = [(out_ref, d) for out_ref in out_refs for d in range(out_ref.shape[0])]
    brings = [
        pltpu.make_async_copy(in_refs[which].at[e], held.at[d], in_sems.at[d])
        for d, (which, e) in enumerate(sources)
    ]
    puts = [pltpu.make_async_copy(held.at[d], out.at[e], out_sems.at[d]) for d, (out, e) in enumerate(places)]
    for bring in brings:
        bring.start()
    for bring, put in zip(brings, puts):
        bring.wait()
        put.start()
    for put in puts:
        put.wait()


def move_blocks(inputs, sources, parts, index, name):
    shape, count = inputs[0].shape[1:], len(sources)
    return pl.pallas_call(
        functools.partial(move_body, sources),
        in_specs=[pl.BlockSpec(memory_space=pltpu.SMEM)] + [pl.BlockSpec(memory_space=pl.ANY)] * len(inputs),
        out_specs=[pl.BlockSpec(memory_space=pl.ANY)] * len(parts),
        out_shape=[jax.ShapeDtypeStruct((part, *shape), jnp.float32) for part in parts],
        scratch_shapes=[
            pltpu.VMEM((count, *shape), jnp.float32),
            pltpu.SemaphoreType.DMA((count,)),
            pltpu.SemaphoreType.DMA((count,)),
        ],
        name=name,
        compiler_params=pltpu.CompilerParams(vmem_limit_bytes=LARGE),
        cost_estimate=pl.CostEstimate(flops=0, bytes_accessed=8 * count * shape[0] * shape[1], transcendentals=0),
    )(index, *inputs)


def split_body(cut, index_ref, own_ref, one_ref, two_ref, high_ref, low_ref):
    del index_ref
    deep = own_ref.shape[1]
    high_ref[0, :, :deep], low_ref[0, :, :deep] = split(own_ref[...])
    other = jnp.where(pl.program_id(0) < cut, one_ref[0], two_ref[0])
    high_ref[0, :, deep:], low_ref[0, :, deep:] = split(other)


def split_slab(a_stored, index, one, two):
    cut, rows, deep = one.shape
    count = cut + two.shape[0]
    out = jax.ShapeDtypeStruct((count, rows, 2 * deep), jnp.bfloat16)
    out_spec = pl.BlockSpec((1, rows, 2 * deep), lambda g, index: (g, 0, 0))
    return pl.pallas_call(
        functools.partial(split_body, cut),
        grid_spec=pltpu.PrefetchScalarGridSpec(
            num_scalar_prefetch=1,
            grid=(count,),
            in_specs=[
                pl.BlockSpec((rows, deep), lambda g, index: (0, index[g])),
                pl.BlockSpec((1, rows, deep), lambda g, index: (jnp.minimum(g, cut - 1), 0, 0)),
                pl.BlockSpec((1, rows, deep), lambda g, index: (jnp.maximum(g - cut, 0), 0, 0)),
            ],
            out_specs=[out_spec, out_spec],
        ),
        out_shape=[out, out],
        name="split_slab",
        compiler_params=pltpu.CompilerParams(vmem_limit_bytes=SMALL),
        cost_estimate=pl.CostEstimate(flops=0, bytes_accessed=16 * count * rows * deep, transcendentals=0),
    )(index, a_stored, one, two)


def product_body(cut, first, ordered, has_start, place_ref, *refs):
    out_ref = refs[-1]
    at = pl.program_id(0)
    at = at if ordered else place_ref[first + at]
    dot = functools.partial(jnp.dot, preferred_element_type=jnp.float32)
    own_ref, other_ref, one_ref, two_ref = refs[:4]
    rights = [own_ref[0], other_ref[0], jnp.where(at < cut, one_ref[0], two_ref[0])]
    total = refs[10][0] if has_start else None
    for t, right in enumerate(rights):
        left_high, left_low = refs[4 + 2 * t : 6 + 2 * t]
        high, low = split(right)
        part = dot(left_high[0], high) + (dot(left_high[0], low) + dot(left_low[0], high))
        total = part if total is None else total + part
    out_ref[0] = total


def products(place, a_high, a_low, panels, first, count, base=None, start=None):
    own, other, one, two = panels
    deep, cols = own.shape[1:]
    rows, cut = a_high.shape[1], one.shape[0]
    ordered = base is not None

    def left_at(term):
        return lambda g, place: (place[first + g] + place[len(OFFSETS) + term], 0, 0)

    def right_at(offset, low, high):
        def at(g, place):
            index = g + offset if ordered else place[first + g]
            return (jnp.clip(index - low, 0, high - 1), 0, 0)

        return at

    block = (1, deep, cols)
    in_specs = [
        pl.BlockSpec(block, right_at(base or 0, 0, own.shape[0])),
        pl.BlockSpec(block, right_at(base or 0, 0, other.shape[0])),
        pl.BlockSpec(block, right_at(0, 0, cut)),
        pl.BlockSpec(block, right_at(0, cut, two.shape[0])),
    ]
    for term in range(WINDOW):
        in_specs += [pl.BlockSpec((1, rows, deep), left_at(term))] * 2
    args = [own, other, one, two] + [a_high, a_low] * WINDOW
    if start is not None:
        in_specs += [pl.BlockSpec((1, rows, cols), lambda g, place: (first + g, 0, 0))]
        args += [start]
    blocks = count * WINDOW
    return pl.pallas_call(
        functools.partial(product_body, cut, first, ordered, start is not None),
        grid_spec=pltpu.PrefetchScalarGridSpec(
            num_scalar_prefetch=1,
            grid=(count,),
            in_specs=in_specs,
            out_specs=pl.BlockSpec((1, rows, cols), lambda g, place: (g, 0, 0)),
        ),
        out_shape=jax.ShapeDtypeStruct((count, rows, cols), jnp.float32),
        name="products",
        compiler_params=pltpu.CompilerParams(vmem_limit_bytes=SMALL),
        cost_estimate=pl.CostEstimate(
            flops=6 * blocks * rows * deep * cols, bytes_accessed=8 * blocks * deep * cols, transcendentals=0
        ),
    )(place, *args)


def shifted(block, axes, distance):
    n = lax.axis_size(axes)
    return lax.ppermute(block, axes, [((i - distance) % n, i) for i in range(n)])


def to_other_core(block):
    return lax.ppermute(block, ROW, [(i, i ^ 1) for i in range(lax.axis_size(ROW))])


def to_next_chips(own, other):
    n = lax.axis_size(ROW)
    one = lax.ppermute(own, ROW, [(i, (i + (1 if i % 2 else -1)) % n) for i in range(n)])
    two = lax.ppermute(other, ROW, [(i, (i + (-2 if i % 2 else 2)) % n) for i in range(n)])
    return one, two


def exchange(block, axes):
    return lax.all_to_all(block, axes, split_axis=0, concat_axis=0, tiled=True)


def on_device(a_stored, b_stored):
    blocks = lax.axis_size(ROW)
    planes = lax.axis_size("z")
    deep = b_stored.shape[0] // blocks
    row_index = lax.axis_index(ROW).astype(jnp.int32)
    col_index = lax.axis_index(COL).astype(jnp.int32)
    plane = lax.axis_index("z").astype(jnp.int32)
    side = lax.axis_index("y_lo").astype(jnp.int32)
    kinds = jnp.arange(planes + WINDOW - 1, dtype=jnp.int32)
    mine = (row_index + side * planes + kinds) % blocks
    theirs = (row_index + (1 - side) * planes + kinds) % blocks
    around = (plane + jnp.array(OFFSETS, dtype=jnp.int32)) % planes
    core = lax.axis_index("core").astype(jnp.int32)
    place = jnp.concatenate([around, jnp.stack([jnp.ones_like(core), 2 - 2 * core, 2 * core])])
    half = deep // 2
    y_hi, x = lax.axis_index("y_hi").astype(jnp.int32), lax.axis_index("x").astype(jnp.int32)
    x_count = lax.axis_size("x")

    order = (jnp.arange(blocks, dtype=jnp.int32) + col_index + 1) % blocks
    (panel,) = order_blocks(b_stored, 2 * order, half, 0, (blocks,), "order_panel")

    step = jnp.arange(blocks, dtype=jnp.int32)
    to_core, to_y, to_x = step // (2 * x_count) ^ core, step // x_count % 2 ^ y_hi, (step % x_count + x) % x_count
    far = (to_y * planes + to_x * 2 + to_core + col_index + 1) % blocks
    far, panel = lax.optimization_barrier((far, panel))
    here, there = order_blocks(b_stored, 2 * far + 1, half, 0, (planes, planes), "order_panel")
    there = to_other_core(there)
    slab = jnp.concatenate([2 * theirs, 2 * theirs + 1])
    slab, panel = lax.optimization_barrier((slab, panel))
    kinds = kinds.shape[0]
    slabs = list(order_blocks(a_stored, slab, half, 1, (EARLY, kinds - EARLY, LATE, kinds - LATE), "order_slab"))
    here_across = shifted(here[x_count:], "y_hi", 1)
    panel = exchange(panel, ROW)
    slabs[0] = shifted(slabs[0], "y_lo", 1)
    panel, here_across, *slabs = lax.optimization_barrier((panel, here_across, *slabs))

    pieces = (step % 2 ^ side) * planes + step // 2
    (one,) = order_blocks(panel.reshape(-1, panel.shape[2]), pieces, half, 0, (blocks,), "order_planes")
    there, one = lax.optimization_barrier((there, one))
    there_across = shifted(there[x_count:], "y_hi", 1)
    there_across, *slabs = lax.optimization_barrier((there_across, *slabs))
    slabs[1:3] = [shifted(slab, "y_lo", 1) for slab in slabs[1:3]]
    held = [here, here_across, there, there_across]
    sources = tuple((which, distance) for distance in range(x_count) for which in range(4))
    along = move_blocks(held, sources, (4,) * x_count, step, "order_distance")
    along = [along[0]] + [shifted(along[d], "x", d) for d in range(1, x_count)]
    from_x, from_core, from_y = (x - step // 4) % x_count, step // 2 % 2 ^ core, step % 2 ^ y_hi
    goal = (from_x * 2 + from_core) * 2 + (from_y ^ side)
    sources = tuple((distance, e) for distance in range(x_count) for e in range(4))
    (two,) = move_blocks(along, sources, (blocks,), goal, "order_planes")
    one, two = one.reshape(planes, deep, -1), two.reshape(planes, deep, -1)

    one = exchange(one, "z")
    two, one, *slabs = lax.optimization_barrier((two, one, *slabs))
    slabs[3] = shifted(slabs[3], "y_lo", 1)
    one_other = to_other_core(one)
    one_next = to_next_chips(one[: planes // 2], one_other[planes // 2 :])
    two = exchange(two, "z")
    a_first = split_slab(a_stored, 2 * mine, *slabs[:2])
    total = products(place, *a_first, [one, one_other, *one_next], 0, planes)
    total, *slabs = lax.optimization_barrier((total, *slabs))
    a_second = split_slab(a_stored, 2 * mine + 1, *slabs[2:])

    two, total, *a_second = lax.optimization_barrier((two, total, *a_second))
    groups = order_blocks(two.reshape(-1, two.shape[2]), around, deep, 0, GROUPS, "order_rest", SMALL)
    others = [to_other_core(group) for group in groups]
    done, first = [], 0
    for own, other, count in zip(groups, others, GROUPS):
        came = to_next_chips(own[: count // 2], other[count // 2 :])
        part = products(place, *a_second, [own, other, *came], first, count, 0, total)
        done += [part[g] for g in range(count)]
        first += count
    ahead, behind = shifted(done[0], "z", 1), shifted(done[1], "z", -1)
    for far in (2, 4):
        ahead = shifted(done[far] + ahead, "z", 1)
        behind = shifted(done[far + 1] + behind, "z", -1)
    ahead = shifted(done[6] + ahead, "z", 1)
    return (done[7] + behind) + ahead


def solution(mesh):
    split_mesh = Mesh(np.array(mesh.devices).reshape(2, 4, 2, 2, 8), AXES)
    return jax.shard_map(
        on_device,
        mesh=split_mesh,
        in_specs=(P(ROW, COL), P(ROW, COL)),
        out_specs=P(ROW, COL),
        check_vma=False,
    )
```
